32 devices in a mesh: groups: 2 (over y), tile: 4 (over x, core), tm: 4 (over z).
Axes of the slice: x: 2, y: 2, z: 4, core: 2. Of those that a mesh axis runs over, the one named last changes fastest.
Arguments:
- frames: float32 [2048, 8192], P(('groups', 'tm'), 'tile'), parts along dimension 0
- segment_ids: int32 [2048], P(('groups', 'tm')), parts along dimension 0, may hold values from 0 to 7, never falling along the last dimension, each value on 1 to 512 neighbouring positions
Outputs:
- instant_cov: float32 [16384, 8192], P(('groups', 'tile'), 'tm'), parts along dimension 0
- lagged_cov: float32 [16384, 8192], P(('groups', 'tile'), 'tm'), parts along dimension 0
The draws below stay inside these ranges and needn't reach their ends.
There are 2 independent parts, one for each index of `groups`. The reference program is written for one: setup_inputs(seed, part) draws one part's arguments, and reference() takes and returns one part's arrays. A program takes and returns all parts, laid end to end along the dimension named above; each array names one. Nothing has to cross between parts.
Inputs may be any that keep to these rules, and one draw needn't show every extreme that they name: `segment_ids`: never falling along the frames; each segment has at most 512 frames, and one has exactly that many.
All inputs are finite; a program needn't handle non-finite values.
Results may differ from the reference program's by a relative error of at most 0.0021.
Values may be sent and summed in bfloat16 or wider, within the bound.
A program may use at most 128 MiB of HBM per device.

```python
import math
import jax
import jax.numpy as jnp
import numpy as np
from jax import lax

F = 8192
LAG = 100
SEGMENTS = 8
NFRAMES = 1024


def draw_frames(key, part):
    key = jax.random.fold_in(key, 11)
    keys = jax.random.split(key, 6)
    times = jnp.arange(NFRAMES, dtype=jnp.float32)
    which = jnp.arange(F, dtype=jnp.int32) % 8
    omega = jnp.exp(jax.random.uniform(keys[0], (8,), jnp.float32, jnp.log(0.005), jnp.log(0.2)))
    phase = jax.random.uniform(keys[1], (8,), jnp.float32, -3.14159, 3.14159)
    signal = jnp.sin(times[:, None] * omega[None, :] + phase[None, :])
    loading = jax.random.normal(keys[2], (F,), jnp.float32)
    offset = jax.random.uniform(keys[3], (F,), jnp.float32, -2.0, 2.0)
    scale = jnp.exp(jax.random.uniform(keys[4], (F,), jnp.float32, jnp.log(0.3), jnp.log(3.0)))
    noise = jax.random.normal(keys[5], (NFRAMES, F), jnp.float32)
    shared = signal[:, which] * loading[None, :]
    return offset[None, :] + scale[None, :] * (noise + 0.8 * shared)


def length_profile(number_of, total, limit, slope):
    weights = [(1 << 20) // math.isqrt(grade ** slope) + 1 for grade in range(2, number_of + 1)]
    rest, given = total - limit - (number_of - 1), [1] * (number_of - 1)
    while rest > 0:
        free = [i for i in range(number_of - 1) if given[i] < limit]
        pool, remaining = sum([weights[i] for i in free]), rest
        for i in free:
            more = min(limit - given[i], max(1, remaining * weights[i] // pool), rest)
            given[i] = given[i] + more
            rest = rest - more
    return np.array([limit] + given)


def uneven(own_key, count, total, limit, lean):
    if count == 2:
        one = jax.random.randint(own_key, (), max(1, total - limit), min(limit, total - 1) + 1)
        return jnp.stack([one, total - one])
    sizes = jnp.asarray(length_profile(count, total, limit, lean), jnp.int32)
    twos = (count - 1) // 2
    donor, taker = sizes[1:1 + 2 * twos:2], sizes[2:2 + 2 * twos:2]
    slack = jnp.minimum(donor - 1, limit - taker)
    moved = jax.random.randint(jax.random.fold_in(own_key, 1), (twos,), 0, 1 << 20) % (slack + 1)
    sizes = sizes.at[1:1 + 2 * twos:2].set(donor - moved).at[2:2 + 2 * twos:2].set(taker + moved)
    return sizes[jax.random.permutation(jax.random.fold_in(own_key, 2), count)]


def setup_inputs(seed: int = 0, part: int = 0) -> dict:
    key_of = jax.random.split(jax.random.key(seed), 3)
    part_keys = jax.random.split(jax.random.fold_in(key_of[2], part), 3)
    return {
        "frames": draw_frames(jax.random.fold_in(jax.random.fold_in(key_of[2], part), 71), part),
        "segment_ids": jnp.searchsorted(jnp.cumsum(uneven(part_keys[1], SEGMENTS, NFRAMES, NFRAMES // 2, 1)), jnp.arange(NFRAMES), side="right").astype(jnp.int32),
    }


def reference(frames, segment_ids):
    total = frames.shape[0]
    width = frames.shape[1]
    later = jnp.concatenate([frames[LAG:], jnp.zeros((LAG, width), jnp.float32)], axis=0)
    later_seg = jnp.concatenate([segment_ids[LAG:], jnp.full((LAG,), -1, jnp.int32)], axis=0)
    places = jnp.arange(total, dtype=jnp.int32)
    weight = ((segment_ids == later_seg) & (places + LAG < total)).astype(jnp.float32)
    pair_count = jnp.sum(weight)
    center = (jnp.sum(weight[:, None] * frames, axis=0) + jnp.sum(weight[:, None] * later, axis=0)) / (2.0 * pair_count)
    early = (weight[:, None] * (frames - center[None, :])).astype(jnp.bfloat16)
    late = (weight[:, None] * (later - center[None, :])).astype(jnp.bfloat16)
    stacked = jnp.concatenate([early, late], axis=0)
    swapped = jnp.concatenate([late, early], axis=0)
    block_rows = 1024
    row_blocks = width // block_rows if width % block_rows == 0 else 1
    if row_blocks == 1:
        block_rows = width

    def one_block(index):
        left = lax.dynamic_slice_in_dim(stacked, index * block_rows, block_rows, 1)
        inst = lax.dot_general(left, stacked, (((0,), (0,)), ((), ())), preferred_element_type=jnp.float32)
        lagd = lax.dot_general(left, swapped, (((0,), (0,)), ((), ())), preferred_element_type=jnp.float32)
        return inst, lagd

    inst_blocks, lag_blocks = lax.map(one_block, jnp.arange(row_blocks, dtype=jnp.int32))
    instant_cov = inst_blocks.reshape(width, width) / (2.0 * pair_count)
    lagged_cov = lag_blocks.reshape(width, width) / (2.0 * pair_count)
    return instant_cov, lagged_cov
```

```python
import functools

import jax
import jax.numpy as jnp
from jax import lax
from jax.experimental import pallas as pl
from jax.experimental.pallas import tpu as pltpu
from jax.sharding import PartitionSpec as P

LAG = 100
LANES = 128
PIECES = 2
MESH = pl.DeviceIdType.MESH


def aligned(value, step):
    return pl.multiple_of(value, step)


def gather_kernel(
    n, tiles, pc,
    frames_ref, seg_ref,
    sum_t_ref, dif_t_ref, cols_ref, weight_ref, scale_ref,
    rows, seg_all, v_all, sums_all,
    seg_send, seg_recv, tot_send, tot_recv,
    up_send, down_send, row_recv, xup_send, xdown_send, sib_send, col_recv, own_sem,
):
    slab_rows, width = frames_ref.shape
    total = n * slab_rows
    piece = slab_rows // PIECES
    z = lax.axis_index("tm")
    t = lax.axis_index("tile")
    x, core = t // 2, t % 2
    sibling = x * 2 + (1 - core)
    last_x = tiles // 2 - 1
    right, left = (t + 2) % tiles, (t + tiles - 2) % tiles

    barrier = pltpu.get_barrier_semaphore()
    for step in range(1, n):
        pl.semaphore_signal(barrier, inc=1, device_id={"tm": (z + step) % n}, device_id_type=MESH)
    for other in (sibling, right, left):
        pl.semaphore_signal(barrier, inc=1, device_id={"tile": other}, device_id_type=MESH)
    pl.semaphore_wait(barrier, n - 1 + 3)

    def to_all(buffer, send, recv):
        return [
            pltpu.make_async_remote_copy(
                src_ref=buffer.at[z], dst_ref=buffer.at[z],
                send_sem=send.at[step], recv_sem=recv.at[step],
                device_id={"tm": (z + step) % n}, device_id_type=MESH,
            )
            for step in range(1, n)
        ]

    seg_all[z] = seg_ref[...]
    copies = to_all(seg_all, seg_send, seg_recv)
    for copy in copies:
        copy.start()
    rows[total:, :] = jnp.zeros((LANES, width), jnp.bfloat16)
    for copy in copies:
        copy.wait()
    seg = jnp.concatenate([seg_all[slab] for slab in range(n)], axis=1)
    places = lax.broadcasted_iota(jnp.int32, seg.shape, 1)
    same = (seg == pltpu.roll(seg, total - LAG, 1)) & (places + LAG < total)
    weight = jnp.where(same, 1.0, 0.0).astype(jnp.float32)
    pairs = jnp.sum(weight, axis=1, keepdims=True)
    uses = weight + pltpu.roll(weight, LAG, 1)
    for slab in range(n):
        v_all[slab] = uses[:, slab * slab_rows : (slab + 1) * slab_rows]
    scale_ref[...] = jnp.broadcast_to(0.25 / pairs, scale_ref.shape)

    parts = width // LANES
    local = jnp.dot(
        v_all[z], frames_ref[...],
        precision=lax.Precision.HIGHEST, preferred_element_type=jnp.float32,
    )
    for part in range(parts):
        sums_all[z, part : part + 1, :] = local[0:1, part * LANES : (part + 1) * LANES]
    copies = to_all(sums_all, tot_send, tot_recv)
    for copy in copies:
        copy.start()
    for slab in range(n):
        column = weight[0:1, slab * slab_rows : (slab + 1) * slab_rows]
        weight_ref[slab * slab_rows : (slab + 1) * slab_rows, :] = jnp.broadcast_to(
            column, (LANES, slab_rows)
        ).T
    for copy in copies:
        copy.wait()
    sums = sums_all[0]
    for slab in range(1, n):
        sums = sums + sums_all[slab]
    center = sums / (2.0 * pairs[0:1, 0:1])

    def span(slab, k):
        return pl.ds(aligned(slab * slab_rows + k * piece, piece), piece)

    def row_copy(slab, k, up):
        here = rows.at[span(slab, k)]
        return pltpu.make_async_remote_copy(
            src_ref=here, dst_ref=here,
            send_sem=(up_send if up else down_send).at[slab, k],
            recv_sem=row_recv.at[slab, k],
            device_id={"tm": jnp.minimum(z + 1, n - 1) if up else jnp.maximum(z - 1, 0)},
            device_id_type=MESH,
        )

    def col_copy(m, slab, k, where, source):
        there = cols_ref.at[m, span(slab, k)]
        send, dev = {
            "sib": (sib_send, sibling),
            "up": (xup_send, right),
            "down": (xdown_send, left),
        }[where]
        return pltpu.make_async_remote_copy(
            src_ref=rows.at[span(slab, k)] if source else there, dst_ref=there,
            send_sem=send.at[m, slab, k], recv_sem=col_recv.at[m, slab, k],
            device_id={"tile": dev}, device_id_type=MESH,
        )

    def own_copy(m, slab, k):
        return pltpu.make_async_copy(
            rows.at[span(slab, k)], cols_ref.at[m, span(slab, k)], own_sem.at[m, slab, k]
        )

    def roles(m):
        source = z * pc + m
        is_source = t == source
        relay = (core == source % 2) & (t != source)
        goes_up = (x < last_x) & (x >= source // 2)
        goes_down = (x > 0) & (x <= source // 2)
        return is_source, relay, goes_up, goes_down

    def each_column(slab, k, from_rows, act):
        for m in range(pc):
            is_source, relay, goes_up, goes_down = roles(m)
            if from_rows:
                @pl.when(is_source)
                def _():
                    own = own_copy(m, slab, k)
                    own.start() if act is start else own.wait()
                    act(col_copy(m, slab, k, "sib", True))

                @pl.when(is_source & goes_up)
                def _():
                    act(col_copy(m, slab, k, "up", True))

                @pl.when(is_source & goes_down)
                def _():
                    act(col_copy(m, slab, k, "down", True))
            else:
                @pl.when(relay & goes_up)
                def _():
                    act(col_copy(m, slab, k, "up", False))

                @pl.when(relay & goes_down)
                def _():
                    act(col_copy(m, slab, k, "down", False))

                @pl.when(relay)
                def _():
                    act(col_copy(m, slab, k, "sib", False))

    start = lambda copy: copy.start()

    sent = lambda copy: copy.wait_send()

    def column_arrives(slab, k):
        for m in range(pc):
            is_source = roles(m)[0]

            @pl.when(jnp.logical_not(is_source))
            def _():
                col_copy(m, slab, k, "sib", False).wait_recv()

        each_column(slab, k, False, start)

    def prepare(slab):
        base = aligned(slab * slab_rows, slab_rows)
        w = weight_ref[pl.ds(base, slab_rows), :]

        @pl.loop(0, parts)
        def _(part):
            at = aligned(part * LANES, LANES)
            c = rows[pl.ds(base, slab_rows + LANES), pl.ds(at, LANES)].astype(jnp.float32)
            now = c[:slab_rows]
            lagged = pltpu.roll(c, slab_rows + LANES - LAG, 0)[:slab_rows]
            sum_t_ref[pl.ds(at, LANES), pl.ds(base, slab_rows)] = (
                (w * (now + lagged)).T.astype(jnp.bfloat16)
            )
            dif_t_ref[pl.ds(at, LANES), pl.ds(base, slab_rows)] = (
                (w * (now - lagged)).T.astype(jnp.bfloat16)
            )

    for k in range(PIECES):
        for part in range(parts):
            at = slice(part * LANES, (part + 1) * LANES)
            rows[span(z, k), at] = (
                frames_ref[k * piece : (k + 1) * piece, at] - center[part : part + 1, :]
            ).astype(jnp.bfloat16)

        @pl.when(z < n - 1)
        def _():
            row_copy(z, k, True).start()

        @pl.when(z > 0)
        def _():
            row_copy(z, k, False).start()

        each_column(z, k, True, start)

    def row_arrives(d, k):
        below, above = z - d, z + d

        @pl.when(below >= 0)
        def _():
            row_copy(below, k, True).wait_recv()

            @pl.when(z < n - 1)
            def _():
                row_copy(below, k, True).start()

            each_column(below, k, True, start)

        @pl.when(above < n)
        def _():
            row_copy(above, k, False).wait_recv()

            @pl.when(z > 0)
            def _():
                row_copy(above, k, False).start()

            each_column(above, k, True, start)

    def columns_arrive(d, k):
        if d == 0:
            column_arrives(z, k)
            return

        @pl.when(z - d >= 0)
        def _():
            column_arrives(z - d, k)

        @pl.when(z + d < n)
        def _():
            column_arrives(z + d, k)

    steps = [(d, k) for d in range(n) for k in range(PIECES)]
    behind = 0
    for index, (d, k) in enumerate(steps):
        if d > 0:
            row_arrives(d, k)
            columns_arrive(*steps[behind])
            behind += 1
        if k == PIECES - 1:
            if d > 0:
                @pl.when(z - d >= 0)
                def _():
                    prepare(z - d)

                @pl.when(z + d < n)
                def _():
                    prepare(z + d - 1)

            @pl.when(z + d == n - 1)
            def _():
                prepare(n - 1)

    for entry in steps[behind:]:
        columns_arrive(*entry)

    for slab in range(n):
        for k in range(PIECES):
            @pl.when((z < n - 1) & (slab <= z))
            def _():
                row_copy(slab, k, True).wait_send()

            @pl.when((z > 0) & (slab >= z))
            def _():
                row_copy(slab, k, False).wait_send()

            each_column(slab, k, True, sent)
            each_column(slab, k, False, sent)


def product_kernel(sum_t_ref, dif_t_ref, cols_ref, weight_ref, scale_ref, inst_ref, lag_ref, plus, minus):
    total, wide = plus.shape
    for part in range(wide // LANES):
        at = slice(part * LANES, (part + 1) * LANES)
        c = cols_ref[0, :, at].astype(jnp.float32)
        lagged = pltpu.roll(c, total - LAG, 0)
        w = weight_ref[...]
        plus[:, at] = (w * (c + lagged)).astype(jnp.bfloat16)
        minus[:, at] = (w * (c - lagged)).astype(jnp.bfloat16)
    height = sum_t_ref.shape[0]
    block = min(512, height)
    scale = scale_ref[0:1, 0:1]
    for index in range(height // block):
        at = slice(index * block, (index + 1) * block)
        a = jnp.dot(sum_t_ref[at, :], plus[...], preferred_element_type=jnp.float32)
        b = jnp.dot(dif_t_ref[at, :], minus[...], preferred_element_type=jnp.float32)
        inst_ref[at, :] = (a + b) * scale
        lag_ref[at, :] = (a - b) * scale


def body(frames, segment_ids):
    n, tiles = lax.axis_size("tm"), lax.axis_size("tile")
    pc = tiles // n
    slab_rows, width = frames.shape
    total = n * slab_rows
    sum_rows = -(-(width // LANES) // 8) * 8
    seg = jnp.broadcast_to(segment_ids[None, :], (8, slab_rows))
    vmem = pl.BlockSpec(memory_space=pltpu.VMEM)
    dma = pltpu.SemaphoreType.DMA
    sum_t, dif_t, cols, weight, scale = pl.pallas_call(
        functools.partial(gather_kernel, n, tiles, pc),
        out_shape=(
            jax.ShapeDtypeStruct((width, total), jnp.bfloat16),
            jax.ShapeDtypeStruct((width, total), jnp.bfloat16),
            jax.ShapeDtypeStruct((pc, total, width), jnp.bfloat16),
            jax.ShapeDtypeStruct((total, LANES), jnp.float32),
            jax.ShapeDtypeStruct((8, LANES), jnp.float32),
        ),
        in_specs=[vmem, vmem],
        out_specs=(vmem, vmem, pl.BlockSpec(memory_space=pl.ANY), vmem, vmem),
        scratch_shapes=[
            pltpu.VMEM((total + LANES, width), jnp.bfloat16),
            pltpu.VMEM((n, 8, slab_rows), jnp.int32),
            pltpu.VMEM((n, 8, slab_rows), jnp.float32),
            pltpu.VMEM((n, sum_rows, LANES), jnp.float32),
            dma((n,)), dma((n,)), dma((n,)), dma((n,)),
            dma((n, PIECES)), dma((n, PIECES)), dma((n, PIECES)),
            dma((pc, n, PIECES)), dma((pc, n, PIECES)), dma((pc, n, PIECES)),
            dma((pc, n, PIECES)), dma((pc, n, PIECES)),
        ],
        compiler_params=pltpu.CompilerParams(
            collective_id=0, has_side_effects=True, vmem_limit_bytes=44 * 1024 * 1024
        ),
    )(frames, seg)

    wide = min(256, width)
    per_tile = width // wide
    out = jax.ShapeDtypeStruct((width, pc * width), jnp.float32)
    whole = pl.BlockSpec((width, total), lambda j: (0, 0))
    tile = pl.BlockSpec((width, wide), lambda j: (0, j))
    return pl.pallas_call(
        product_kernel,
        grid=(pc * per_tile,),
        out_shape=(out, out),
        in_specs=[
            whole, whole,
            pl.BlockSpec((1, total, wide), lambda j: (j // per_tile, 0, j % per_tile)),
            pl.BlockSpec((total, LANES), lambda j: (0, 0)),
            pl.BlockSpec((8, LANES), lambda j: (0, 0)),
        ],
        out_specs=(tile, tile),
        scratch_shapes=[pltpu.VMEM((total, wide), jnp.bfloat16)] * 2,
        compiler_params=pltpu.CompilerParams(vmem_limit_bytes=44 * 1024 * 1024),
        cost_estimate=pl.CostEstimate(
            flops=4 * total * width * width * pc,
            bytes_accessed=8 * width * width * pc + 6 * total * width,
            transcendentals=0,
        ),
    )(sum_t, dif_t, cols, weight, scale)


def solution(mesh):
    return jax.shard_map(
        body,
        mesh=mesh,
        in_specs=(P(("groups", "tm"), "tile"), P(("groups", "tm"))),
        out_specs=(P(("groups", "tile"), "tm"), P(("groups", "tile"), "tm")),
        check_vma=False,
    )
```

```python
import functools

import jax
import jax.numpy as jnp
from jax import lax
from jax.experimental import pallas as pl
from jax.experimental.pallas import tpu as pltpu
from jax.sharding import PartitionSpec as P

LAG = 100
LANES = 128
PIECES = 4
MESH = pl.DeviceIdType.MESH


def aligned(value, step):
    return pl.multiple_of(value, step)


def gather_kernel(
    n, tiles, pc,
    frames_ref, seg_ref,
    sum_t_ref, dif_t_ref, cols_ref, weight_ref, scale_ref,
    rows, seg_all, v_all, sums_all,
    seg_send, seg_recv, tot_send, tot_recv,
    up_send, down_send, row_recv, xup_send, xdown_send, sib_send, col_recv, own_sem,
):
    slab_rows, width = frames_ref.shape
    total = n * slab_rows
    piece = slab_rows // PIECES
    z = lax.axis_index("tm")
    t = lax.axis_index("tile")
    x, core = t // 2, t % 2
    sibling = x * 2 + (1 - core)
    last_x = tiles // 2 - 1
    right, left = (t + 2) % tiles, (t + tiles - 2) % tiles

    barrier = pltpu.get_barrier_semaphore()
    for step in range(1, n):
        pl.semaphore_signal(barrier, inc=1, device_id={"tm": (z + step) % n}, device_id_type=MESH)
    for other in (sibling, right, left):
        pl.semaphore_signal(barrier, inc=1, device_id={"tile": other}, device_id_type=MESH)
    pl.semaphore_wait(barrier, n - 1 + 3)

    def to_all(buffer, send, recv):
        return [
            pltpu.make_async_remote_copy(
                src_ref=buffer.at[z], dst_ref=buffer.at[z],
                send_sem=send.at[step], recv_sem=recv.at[step],
                device_id={"tm": (z + step) % n}, device_id_type=MESH,
            )
            for step in range(1, n)
        ]

    seg_all[z] = seg_ref[...]
    copies = to_all(seg_all, seg_send, seg_recv)
    for copy in copies:
        copy.start()
    rows[total:, :] = jnp.zeros((LANES, width), jnp.bfloat16)
    for copy in copies:
        copy.wait()
    seg = jnp.concatenate([seg_all[slab] for slab in range(n)], axis=1)
    places = lax.broadcasted_iota(jnp.int32, seg.shape, 1)
    same = (seg == pltpu.roll(seg, total - LAG, 1)) & (places + LAG < total)
    weight = jnp.where(same, 1.0, 0.0).astype(jnp.float32)
    pairs = jnp.sum(weight, axis=1, keepdims=True)
    uses = weight + pltpu.roll(weight, LAG, 1)
    for slab in range(n):
        v_all[slab] = uses[:, slab * slab_rows : (slab + 1) * slab_rows]
    scale_ref[...] = jnp.broadcast_to(0.25 / pairs, scale_ref.shape)

    parts = width // LANES
    local = jnp.dot(
        v_all[z], frames_ref[...],
        precision=lax.Precision.HIGHEST, preferred_element_type=jnp.float32,
    )
    for part in range(parts):
        sums_all[z, part : part + 1, :] = local[0:1, part * LANES : (part + 1) * LANES]
    copies = to_all(sums_all, tot_send, tot_recv)
    for copy in copies:
        copy.start()
    for slab in range(n):
        column = weight[0:1, slab * slab_rows : (slab + 1) * slab_rows]
        weight_ref[slab * slab_rows : (slab + 1) * slab_rows, :] = jnp.broadcast_to(
            column, (LANES, slab_rows)
        ).T
    for copy in copies:
        copy.wait()
    sums = sums_all[0]
    for slab in range(1, n):
        sums = sums + sums_all[slab]
    center = sums / (2.0 * pairs[0:1, 0:1])

    def span(slab, k):
        return pl.ds(aligned(slab * slab_rows + k * piece, piece), piece)

    def row_copy(slab, k, up):
        here = rows.at[span(slab, k)]
        return pltpu.make_async_remote_copy(
            src_ref=here, dst_ref=here,
            send_sem=(up_send if up else down_send).at[slab, k],
            recv_sem=row_recv.at[slab, k],
            device_id={"tm": jnp.minimum(z + 1, n - 1) if up else jnp.maximum(z - 1, 0)},
            device_id_type=MESH,
        )

    def col_copy(m, slab, k, where, source):
        there = cols_ref.at[m, span(slab, k)]
        send, dev = {
            "sib": (sib_send, sibling),
            "up": (xup_send, right),
            "down": (xdown_send, left),
        }[where]
        return pltpu.make_async_remote_copy(
            src_ref=rows.at[span(slab, k)] if source else there, dst_ref=there,
            send_sem=send.at[m, slab, k], recv_sem=col_recv.at[m, slab, k],
            device_id={"tile": dev}, device_id_type=MESH,
        )

    def own_copy(m, slab, k):
        return pltpu.make_async_copy(
            rows.at[span(slab, k)], cols_ref.at[m, span(slab, k)], own_sem.at[m, slab, k]
        )

    def roles(m):
        source = z * pc + m
        is_source = t == source
        relay = (core == source % 2) & (t != source)
        goes_up = (x < last_x) & (x >= source // 2)
        goes_down = (x > 0) & (x <= source // 2)
        return is_source, relay, goes_up, goes_down

    def each_column(slab, k, from_rows, act):
        for m in range(pc):
            is_source, relay, goes_up, goes_down = roles(m)
            if from_rows:
                @pl.when(is_source)
                def _():
                    own = own_copy(m, slab, k)
                    own.start() if act is start else own.wait()
                    act(col_copy(m, slab, k, "sib", True))

                @pl.when(is_source & goes_up)
                def _():
                    act(col_copy(m, slab, k, "up", True))

                @pl.when(is_source & goes_down)
                def _():
                    act(col_copy(m, slab, k, "down", True))
            else:
                @pl.when(relay & goes_up)
                def _():
                    act(col_copy(m, slab, k, "up", False))

                @pl.when(relay & goes_down)
                def _():
                    act(col_copy(m, slab, k, "down", False))

                @pl.when(relay)
                def _():
                    act(col_copy(m, slab, k, "sib", False))

    start = lambda copy: copy.start()

    sent = lambda copy: copy.wait_send()

    def column_arrives(slab, k):
        for m in range(pc):
            is_source = roles(m)[0]

            @pl.when(jnp.logical_not(is_source))
            def _():
                col_copy(m, slab, k, "sib", False).wait_recv()

        each_column(slab, k, False, start)

    def prepare(slab):
        base = aligned(slab * slab_rows, slab_rows)
        w = weight_ref[pl.ds(base, slab_rows), :]

        @pl.loop(0, parts)
        def _(part):
            at = aligned(part * LANES, LANES)
            c = rows[pl.ds(base, slab_rows + LANES), pl.ds(at, LANES)].astype(jnp.float32)
            now = c[:slab_rows]
            lagged = pltpu.roll(c, slab_rows + LANES - LAG, 0)[:slab_rows]
            sum_t_ref[pl.ds(at, LANES), pl.ds(base, slab_rows)] = (
                (w * (now + lagged)).T.astype(jnp.bfloat16)
            )
            dif_t_ref[pl.ds(at, LANES), pl.ds(base, slab_rows)] = (
                (w * (now - lagged)).T.astype(jnp.bfloat16)
            )

    for k in range(PIECES):
        for part in range(parts):
            at = slice(part * LANES, (part + 1) * LANES)
            rows[span(z, k), at] = (
                frames_ref[k * piece : (k + 1) * piece, at] - center[part : part + 1, :]
            ).astype(jnp.bfloat16)

        @pl.when(z < n - 1)
        def _():
            row_copy(z, k, True).start()

        @pl.when(z > 0)
        def _():
            row_copy(z, k, False).start()

        each_column(z, k, True, start)

    def row_arrives(d, k):
        below, above = z - d, z + d

        @pl.when(below >= 0)
        def _():
            row_copy(below, k, True).wait_recv()

            @pl.when(z < n - 1)
            def _():
                row_copy(below, k, True).start()

            each_column(below, k, True, start)

        @pl.when(above < n)
        def _():
            row_copy(above, k, False).wait_recv()

            @pl.when(z > 0)
            def _():
                row_copy(above, k, False).start()

            each_column(above, k, True, start)

    def columns_arrive(d, k):
        if d == 0:
            column_arrives(z, k)
            return

        @pl.when(z - d >= 0)
        def _():
            column_arrives(z - d, k)

        @pl.when(z + d < n)
        def _():
            column_arrives(z + d, k)

    steps = [(d, k) for d in range(n) for k in range(PIECES)]
    behind, ahead = 0, -(-LANES // piece) - 1
    for index, (d, k) in enumerate(steps):
        if d > 0:
            row_arrives(d, k)
            while behind < index:
                columns_arrive(*steps[behind])
                behind += 1
        if d > 0 and k == ahead:
            @pl.when(z + d < n)
            def _():
                prepare(z + d - 1)

        if k == PIECES - 1:
            if d > 0:
                @pl.when(z - d >= 0)
                def _():
                    prepare(z - d)

            @pl.when(z + d == n - 1)
            def _():
                prepare(n - 1)

    for entry in steps[behind:]:
        columns_arrive(*entry)

    for slab in range(n):
        for k in range(PIECES):
            @pl.when((z < n - 1) & (slab <= z))
            def _():
                row_copy(slab, k, True).wait_send()

            @pl.when((z > 0) & (slab >= z))
            def _():
                row_copy(slab, k, False).wait_send()

            each_column(slab, k, True, sent)
            each_column(slab, k, False, sent)


def product_kernel(
    sum_t_ref, dif_t_ref, first_ref, next_ref, weight_ref, scale_ref, inst_ref, lag_ref,
    plus_0, minus_0, plus_1, minus_1,
):
    total, wide = plus_0.shape
    height = sum_t_ref.shape[0]
    block = min(512, height)
    blocks, parts = height // block, wide // LANES
    scale = scale_ref[0:1, 0:1]
    j = pl.program_id(0)

    def prepare(part, block_ref, plus, minus):
        at = slice(part * LANES, (part + 1) * LANES)
        c = block_ref[0, :, at].astype(jnp.float32)
        lagged = pltpu.roll(c, total - LAG, 0)
        w = weight_ref[...]
        plus[:, at] = (w * (c + lagged)).astype(jnp.bfloat16)
        minus[:, at] = (w * (c - lagged)).astype(jnp.bfloat16)

    def multiply(now, later):
        ready = 0
        for index in range(blocks):
            at = slice(index * block, (index + 1) * block)
            a = jnp.dot(sum_t_ref[at, :], now[0][...], preferred_element_type=jnp.float32)
            b = jnp.dot(dif_t_ref[at, :], now[1][...], preferred_element_type=jnp.float32)
            inst_ref[at, :] = (a + b) * scale
            lag_ref[at, :] = (a - b) * scale
            while ready * blocks < (index + 1) * parts:
                prepare(ready, next_ref, *later)
                ready += 1

    even, odd = (plus_0, minus_0), (plus_1, minus_1)

    @pl.when(j == 0)
    def _():
        for part in range(parts):
            prepare(part, first_ref, *even)

    @pl.when(j % 2 == 0)
    def _():
        multiply(even, odd)

    @pl.when(j % 2 == 1)
    def _():
        multiply(odd, even)


def body(frames, segment_ids):
    n, tiles = lax.axis_size("tm"), lax.axis_size("tile")
    pc = tiles // n
    slab_rows, width = frames.shape
    total = n * slab_rows
    sum_rows = -(-(width // LANES) // 8) * 8
    seg = jnp.broadcast_to(segment_ids[None, :], (8, slab_rows))
    vmem = pl.BlockSpec(memory_space=pltpu.VMEM)
    dma = pltpu.SemaphoreType.DMA
    sum_t, dif_t, cols, weight, scale = pl.pallas_call(
        functools.partial(gather_kernel, n, tiles, pc),
        out_shape=(
            jax.ShapeDtypeStruct((width, total), jnp.bfloat16),
            jax.ShapeDtypeStruct((width, total), jnp.bfloat16),
            jax.ShapeDtypeStruct((pc, total, width), jnp.bfloat16),
            jax.ShapeDtypeStruct((total, LANES), jnp.float32),
            jax.ShapeDtypeStruct((8, LANES), jnp.float32),
        ),
        in_specs=[vmem, vmem],
        out_specs=(vmem, vmem, pl.BlockSpec(memory_space=pl.ANY), vmem, vmem),
        scratch_shapes=[
            pltpu.VMEM((total + LANES, width), jnp.bfloat16),
            pltpu.VMEM((n, 8, slab_rows), jnp.int32),
            pltpu.VMEM((n, 8, slab_rows), jnp.float32),
            pltpu.VMEM((n, sum_rows, LANES), jnp.float32),
            dma((n,)), dma((n,)), dma((n,)), dma((n,)),
            dma((n, PIECES)), dma((n, PIECES)), dma((n, PIECES)),
            dma((pc, n, PIECES)), dma((pc, n, PIECES)), dma((pc, n, PIECES)),
            dma((pc, n, PIECES)), dma((pc, n, PIECES)),
        ],
        compiler_params=pltpu.CompilerParams(
            collective_id=0, has_side_effects=True, vmem_limit_bytes=28 * 1024 * 1024
        ),
    )(frames, seg)

    wide = min(256, width)
    per_tile = width // wide
    out = jax.ShapeDtypeStruct((width, pc * width), jnp.float32)
    whole = pl.BlockSpec((width, total), lambda j: (0, 0))
    last = pc * per_tile - 1

    def next_block(j):
        following = jnp.minimum(j + 1, last)
        return following // per_tile, 0, following % per_tile

    tile = pl.BlockSpec((width, wide), lambda j: (0, j))
    return pl.pallas_call(
        product_kernel,
        grid=(pc * per_tile,),
        out_shape=(out, out),
        in_specs=[
            whole, whole,
            pl.BlockSpec((1, total, wide), lambda j: (0, 0, 0)),
            pl.BlockSpec((1, total, wide), next_block),
            pl.BlockSpec((total, LANES), lambda j: (0, 0)),
            pl.BlockSpec((8, LANES), lambda j: (0, 0)),
        ],
        out_specs=(tile, tile),
        scratch_shapes=[pltpu.VMEM((total, wide), jnp.bfloat16)] * 4,
        compiler_params=pltpu.CompilerParams(vmem_limit_bytes=36 * 1024 * 1024),
        cost_estimate=pl.CostEstimate(
            flops=4 * total * width * width * pc,
            bytes_accessed=8 * width * width * pc + 6 * total * width,
            transcendentals=0,
        ),
    )(sum_t, dif_t, cols, cols, weight, scale)


def solution(mesh):
    return jax.shard_map(
        body,
        mesh=mesh,
        in_specs=(P(("groups", "tm"), "tile"), P(("groups", "tm"))),
        out_specs=(P(("groups", "tile"), "tm"), P(("groups", "tile"), "tm")),
        check_vma=False,
    )
```

```python
import functools

import jax
import jax.numpy as jnp
from jax import lax
from jax.experimental import pallas as pl
from jax.experimental.pallas import tpu as pltpu
from jax.sharding import PartitionSpec as P

LAG = 100
LANES = 128
PIECES = 4
MESH = pl.DeviceIdType.MESH


def aligned(value, step):
    return pl.multiple_of(value, step)


def gather_kernel(
    n, tiles, pc,
    frames_ref, seg_ref,
    sum_t_ref, dif_t_ref, plus_ref, minus_ref, scale_ref,
    rows, cols_ref, weight_ref, seg_all, v_all, sums_all,
    seg_send, seg_recv, tot_send, tot_recv,
    up_send, down_send, row_recv, xup_send, xdown_send, sib_send, col_recv, own_sem,
):
    slab_rows, width = frames_ref.shape
    total = n * slab_rows
    piece = slab_rows // PIECES
    z = lax.axis_index("tm")
    t = lax.axis_index("tile")
    x, core = t // 2, t % 2
    sibling = x * 2 + (1 - core)
    last_x = tiles // 2 - 1
    right, left = (t + 2) % tiles, (t + tiles - 2) % tiles

    barrier = pltpu.get_barrier_semaphore()
    for step in range(1, n):
        pl.semaphore_signal(barrier, inc=1, device_id={"tm": (z + step) % n}, device_id_type=MESH)
    for other in (sibling, right, left):
        pl.semaphore_signal(barrier, inc=1, device_id={"tile": other}, device_id_type=MESH)
    pl.semaphore_wait(barrier, n - 1 + 3)

    def to_all(buffer, send, recv):
        return [
            pltpu.make_async_remote_copy(
                src_ref=buffer.at[z], dst_ref=buffer.at[z],
                send_sem=send.at[step], recv_sem=recv.at[step],
                device_id={"tm": (z + step) % n}, device_id_type=MESH,
            )
            for step in range(1, n)
        ]

    seg_all[z] = seg_ref[...]
    copies = to_all(seg_all, seg_send, seg_recv)
    for copy in copies:
        copy.start()
    rows[total:, :] = jnp.zeros((LANES, width), jnp.bfloat16)
    for m in range(pc):
        cols_ref[m, total:, :] = jnp.zeros((LANES, width), jnp.bfloat16)
    for copy in copies:
        copy.wait()
    seg = jnp.concatenate([seg_all[slab] for slab in range(n)], axis=1)
    places = lax.broadcasted_iota(jnp.int32, seg.shape, 1)
    same = (seg == pltpu.roll(seg, total - LAG, 1)) & (places + LAG < total)
    weight = jnp.where(same, 1.0, 0.0).astype(jnp.float32)
    pairs = jnp.sum(weight, axis=1, keepdims=True)
    uses = weight + pltpu.roll(weight, LAG, 1)
    for slab in range(n):
        v_all[slab] = uses[:, slab * slab_rows : (slab + 1) * slab_rows]
    scale_ref[...] = jnp.broadcast_to(0.25 / pairs, scale_ref.shape)

    parts = width // LANES
    local = jnp.dot(
        v_all[z], frames_ref[...],
        precision=lax.Precision.HIGHEST, preferred_element_type=jnp.float32,
    )
    for part in range(parts):
        sums_all[z, part : part + 1, :] = local[0:1, part * LANES : (part + 1) * LANES]
    copies = to_all(sums_all, tot_send, tot_recv)
    for copy in copies:
        copy.start()
    for slab in range(n):
        column = weight[0:1, slab * slab_rows : (slab + 1) * slab_rows]
        weight_ref[slab * slab_rows : (slab + 1) * slab_rows, :] = jnp.broadcast_to(
            column, (LANES, slab_rows)
        ).T
    for copy in copies:
        copy.wait()
    sums = sums_all[0]
    for slab in range(1, n):
        sums = sums + sums_all[slab]
    center = sums / (2.0 * pairs[0:1, 0:1])

    def span(slab, k):
        return pl.ds(aligned(slab * slab_rows + k * piece, piece), piece)

    def row_copy(slab, k, up):
        here = rows.at[span(slab, k)]
        return pltpu.make_async_remote_copy(
            src_ref=here, dst_ref=here,
            send_sem=(up_send if up else down_send).at[slab, k],
            recv_sem=row_recv.at[slab, k],
            device_id={"tm": jnp.minimum(z + 1, n - 1) if up else jnp.maximum(z - 1, 0)},
            device_id_type=MESH,
        )

    def col_copy(m, slab, k, where, source):
        there = cols_ref.at[m, span(slab, k)]
        send, dev = {
            "sib": (sib_send, sibling),
            "up": (xup_send, right),
            "down": (xdown_send, left),
        }[where]
        return pltpu.make_async_remote_copy(
            src_ref=rows.at[span(slab, k)] if source else there, dst_ref=there,
            send_sem=send.at[m, slab, k], recv_sem=col_recv.at[m, slab, k],
            device_id={"tile": dev}, device_id_type=MESH,
        )

    def own_copy(m, slab, k):
        return pltpu.make_async_copy(
            rows.at[span(slab, k)], cols_ref.at[m, span(slab, k)], own_sem.at[m, slab, k]
        )

    def roles(m):
        source = z * pc + m
        is_source = t == source
        relay = (core == source % 2) & (t != source)
        goes_up = (x < last_x) & (x >= source // 2)
        goes_down = (x > 0) & (x <= source // 2)
        return is_source, relay, goes_up, goes_down

    def each_column(slab, k, from_rows, act):
        for m in range(pc):
            is_source, relay, goes_up, goes_down = roles(m)
            if from_rows:
                @pl.when(is_source)
                def _():
                    if act is start:
                        own_copy(m, slab, k).start()
                    act(col_copy(m, slab, k, "sib", True))

                @pl.when(is_source & goes_up)
                def _():
                    act(col_copy(m, slab, k, "up", True))

                @pl.when(is_source & goes_down)
                def _():
                    act(col_copy(m, slab, k, "down", True))
            else:
                @pl.when(relay & goes_up)
                def _():
                    act(col_copy(m, slab, k, "up", False))

                @pl.when(relay & goes_down)
                def _():
                    act(col_copy(m, slab, k, "down", False))

                @pl.when(relay)
                def _():
                    act(col_copy(m, slab, k, "sib", False))

    start = lambda copy: copy.start()

    sent = lambda copy: copy.wait_send()

    def column_arrives(slab, k):
        for m in range(pc):
            is_source = roles(m)[0]

            @pl.when(is_source)
            def _():
                own_copy(m, slab, k).wait()

            @pl.when(jnp.logical_not(is_source))
            def _():
                col_copy(m, slab, k, "sib", False).wait_recv()

        each_column(slab, k, False, start)

    def prepare(slab):
        base = aligned(slab * slab_rows, slab_rows)
        w = weight_ref[pl.ds(base, slab_rows), :]

        @pl.loop(0, parts)
        def _(part):
            at = aligned(part * LANES, LANES)
            c = rows[pl.ds(base, slab_rows + LANES), pl.ds(at, LANES)].astype(jnp.float32)
            now = c[:slab_rows]
            lagged = pltpu.roll(c, slab_rows + LANES - LAG, 0)[:slab_rows]
            sum_t_ref[pl.ds(at, LANES), pl.ds(base, slab_rows)] = (
                (w * (now + lagged)).T.astype(jnp.bfloat16)
            )
            dif_t_ref[pl.ds(at, LANES), pl.ds(base, slab_rows)] = (
                (w * (now - lagged)).T.astype(jnp.bfloat16)
            )

    def prepare_columns(slab):
        base = aligned(slab * slab_rows, slab_rows)
        w = weight_ref[pl.ds(base, slab_rows), :]
        for m in range(pc):
            @pl.loop(0, parts)
            def _(part):
                at = pl.ds(aligned(part * LANES, LANES), LANES)
                c = cols_ref[m, pl.ds(base, slab_rows + LANES), at].astype(jnp.float32)
                now = c[:slab_rows]
                lagged = pltpu.roll(c, slab_rows + LANES - LAG, 0)[:slab_rows]
                plus_ref[m, pl.ds(base, slab_rows), at] = (w * (now + lagged)).astype(jnp.bfloat16)
                minus_ref[m, pl.ds(base, slab_rows), at] = (w * (now - lagged)).astype(jnp.bfloat16)

    for k in range(PIECES):
        for part in range(parts):
            at = slice(part * LANES, (part + 1) * LANES)
            rows[span(z, k), at] = (
                frames_ref[k * piece : (k + 1) * piece, at] - center[part : part + 1, :]
            ).astype(jnp.bfloat16)

        @pl.when(z < n - 1)
        def _():
            row_copy(z, k, True).start()

        @pl.when(z > 0)
        def _():
            row_copy(z, k, False).start()

        each_column(z, k, True, start)

    def row_arrives(d, k):
        below, above = z - d, z + d

        @pl.when(below >= 0)
        def _():
            row_copy(below, k, True).wait_recv()

            @pl.when(z < n - 1)
            def _():
                row_copy(below, k, True).start()

            each_column(below, k, True, start)

        @pl.when(above < n)
        def _():
            row_copy(above, k, False).wait_recv()

            @pl.when(z > 0)
            def _():
                row_copy(above, k, False).start()

            each_column(above, k, True, start)

    def ready(d, k, form):
        if d > 0 and k == ahead:
            @pl.when(z + d < n)
            def _():
                form(z + d - 1)

        if k == PIECES - 1:
            if d > 0:
                @pl.when(z - d >= 0)
                def _():
                    form(z - d)

            @pl.when(z + d == n - 1)
            def _():
                form(n - 1)

    def columns_arrive(d, k):
        if d == 0:
            column_arrives(z, k)
        else:
            @pl.when(z - d >= 0)
            def _():
                column_arrives(z - d, k)

            @pl.when(z + d < n)
            def _():
                column_arrives(z + d, k)

        ready(d, k, prepare_columns)

    steps = [(d, k) for d in range(n) for k in range(PIECES)]
    behind, ahead = 0, -(-LANES // piece) - 1
    for index, (d, k) in enumerate(steps):
        if d > 0:
            row_arrives(d, k)
            while behind < index:
                columns_arrive(*steps[behind])
                behind += 1
        ready(d, k, prepare)

    for entry in steps[behind:]:
        columns_arrive(*entry)

    for slab in range(n):
        for k in range(PIECES):
            @pl.when((z < n - 1) & (slab <= z))
            def _():
                row_copy(slab, k, True).wait_send()

            @pl.when((z > 0) & (slab >= z))
            def _():
                row_copy(slab, k, False).wait_send()

            each_column(slab, k, True, sent)
            each_column(slab, k, False, sent)


def product_kernel(sum_t_ref, dif_t_ref, plus_ref, minus_ref, scale_ref, inst_ref, lag_ref):
    height = sum_t_ref.shape[0]
    block = min(512, height)
    scale = scale_ref[0:1, 0:1]
    for index in range(height // block):
        at = slice(index * block, (index + 1) * block)
        a = jnp.dot(sum_t_ref[at, :], plus_ref[0], preferred_element_type=jnp.float32)
        b = jnp.dot(dif_t_ref[at, :], minus_ref[0], preferred_element_type=jnp.float32)
        inst_ref[at, :] = (a + b) * scale
        lag_ref[at, :] = (a - b) * scale


def body(frames, segment_ids):
    n, tiles = lax.axis_size("tm"), lax.axis_size("tile")
    pc = tiles // n
    slab_rows, width = frames.shape
    total = n * slab_rows
    sum_rows = -(-(width // LANES) // 8) * 8
    seg = jnp.broadcast_to(segment_ids[None, :], (8, slab_rows))
    vmem = pl.BlockSpec(memory_space=pltpu.VMEM)
    dma = pltpu.SemaphoreType.DMA
    sum_t, dif_t, plus, minus, scale = pl.pallas_call(
        functools.partial(gather_kernel, n, tiles, pc),
        out_shape=(
            jax.ShapeDtypeStruct((width, total), jnp.bfloat16),
            jax.ShapeDtypeStruct((width, total), jnp.bfloat16),
            jax.ShapeDtypeStruct((pc, total, width), jnp.bfloat16),
            jax.ShapeDtypeStruct((pc, total, width), jnp.bfloat16),
            jax.ShapeDtypeStruct((8, LANES), jnp.float32),
        ),
        in_specs=[vmem, vmem],
        out_specs=(vmem, vmem, vmem, vmem, vmem),
        scratch_shapes=[
            pltpu.VMEM((total + LANES, width), jnp.bfloat16),
            pltpu.VMEM((pc, total + LANES, width), jnp.bfloat16),
            pltpu.VMEM((total, LANES), jnp.float32),
            pltpu.VMEM((n, 8, slab_rows), jnp.int32),
            pltpu.VMEM((n, 8, slab_rows), jnp.float32),
            pltpu.VMEM((n, sum_rows, LANES), jnp.float32),
            dma((n,)), dma((n,)), dma((n,)), dma((n,)),
            dma((n, PIECES)), dma((n, PIECES)), dma((n, PIECES)),
            dma((pc, n, PIECES)), dma((pc, n, PIECES)), dma((pc, n, PIECES)),
            dma((pc, n, PIECES)), dma((pc, n, PIECES)),
        ],
        compiler_params=pltpu.CompilerParams(
            collective_id=0, has_side_effects=True, vmem_limit_bytes=28 * 1024 * 1024
        ),
    )(frames, seg)

    wide = min(256, width)
    per_tile = width // wide
    out = jax.ShapeDtypeStruct((width, pc * width), jnp.float32)
    whole = pl.BlockSpec((width, total), lambda j: (0, 0))
    block = pl.BlockSpec((1, total, wide), lambda j: (j // per_tile, 0, j % per_tile))
    tile = pl.BlockSpec((width, wide), lambda j: (0, j))
    return pl.pallas_call(
        product_kernel,
        grid=(pc * per_tile,),
        out_shape=(out, out),
        in_specs=[
            whole, whole,
            block, block,
            pl.BlockSpec((8, LANES), lambda j: (0, 0)),
        ],
        out_specs=(tile, tile),
        compiler_params=pltpu.CompilerParams(vmem_limit_bytes=36 * 1024 * 1024),
        cost_estimate=pl.CostEstimate(
            flops=4 * total * width * width * pc,
            bytes_accessed=8 * width * width * pc + 6 * total * width,
            transcendentals=0,
        ),
    )(sum_t, dif_t, plus, minus, scale)


def solution(mesh):
    return jax.shard_map(
        body,
        mesh=mesh,
        in_specs=(P(("groups", "tm"), "tile"), P(("groups", "tm"))),
        out_specs=(P(("groups", "tile"), "tm"), P(("groups", "tile"), "tm")),
        check_vma=False,
    )
```
